32 devices in a mesh: groups: 2 (over y), tm: 4 (over z), space: 2 (over x), mp: 2 (over core).
Axes of the slice: x: 2, y: 2, z: 4, core: 2. Of those that a mesh axis runs over, the one named last changes fastest.
Arguments:
- query_proj: bfloat16 [16, 16, 8, 2240], P(('groups', 'tm'), 'space', None, 'mp'), parts along dimension 0, may hold values from -6 to 6
- key_proj: bfloat16 [16, 16, 8, 2240], P(('groups', 'tm'), 'space', None, 'mp'), parts along dimension 0, may hold values from -6 to 6
- value_proj: bfloat16 [16, 16, 8, 2240], P(('groups', 'tm'), 'space', None, 'mp'), parts along dimension 0, may hold values from -6 to 6
- expanded: bfloat16 [16, 16, 8, 2, 6720], P(('groups', 'tm'), 'space', None, None, 'mp'), parts along dimension 0, may hold values from -6 to 6
- spatial_weight: float32 [3, 3, 2, 6720], P(None, None, None, 'mp'), may hold values from -0.6 to 0.6
- temporal_weight: float32 [3, 2, 6720], P(None, None, 'mp'), may hold values from -1 to 1
Outputs:
- attended: bfloat16 [16, 16, 8, 2240], P(('groups', 'tm'), 'space', None, 'mp'), parts along dimension 0
- gated_hidden: bfloat16 [16, 16, 8, 6720], P(('groups', 'tm'), 'space', None, 'mp'), parts along dimension 0
The draws below stay inside these ranges and needn't reach their ends.
There are 2 independent parts, one for each index of `groups`. The reference program is written for one: setup_inputs(seed, part) draws one part's arguments, and reference() takes and returns one part's arrays. A program takes and returns all parts, laid end to end along the dimension named above; an argument that names none is the same for every part. Nothing has to cross between parts.
All inputs are finite; a program needn't handle non-finite values.
Results may differ from the reference program's by a relative error of at most 0.0059.
Values may be sent and summed in bfloat16 or wider, within the bound.
A program may use at most 64 MiB of HBM per device.

```python
import jax
import jax.numpy as jnp
from jax import lax

HEADS = 70
HEAD_DIM = 32
FF = 6720
FR_DEV = 2
WIDTH_CELLS = 8
CH = 2240
FRAMES = 8
HEIGHT = 16
N_TM = 4


def block_scale(rng, dims, shards, low, high):
    def one(axis_at, shards_of):
        draws = jax.random.uniform(jax.random.fold_in(jax.random.fold_in(rng, 6), axis_at), (shards_of,), jnp.float32, low / len(shards), high / len(shards))
        return jnp.repeat(jnp.exp(draws), dims[axis_at] // shards_of).reshape((-1,) + (1,) * (len(dims) - axis_at - 1))

    factor_of = one(*shards[0])
    for cut in shards[1:]:
        factor_of = factor_of * one(*cut)
    return factor_of


def gaussian(own_key, shape, scale, reach, pieces=(), kind=jnp.bfloat16):
    array = jax.random.normal(own_key, shape, jnp.float32) * scale
    if len(pieces) > 0:
        array = block_scale(own_key, shape, pieces, -0.22, 0.18) * array
    return jnp.clip(array, min=-reach, max=reach).astype(kind)


def setup_inputs(seed: int = 0, part: int = 0) -> dict:
    key_of = jax.random.split(jax.random.key(seed), 7)
    part_keys = jax.random.split(jax.random.fold_in(key_of[6], part), 7)
    return {
        "query_proj": gaussian(part_keys[0], (FRAMES, HEIGHT, WIDTH_CELLS, CH), 1.0, 6.0, ((0, 4), (1, 2), (3, 2))),
        "key_proj": gaussian(part_keys[1], (FRAMES, HEIGHT, WIDTH_CELLS, CH), 1.0, 6.0, ((0, 4), (1, 2), (3, 2))),
        "value_proj": gaussian(part_keys[2], (FRAMES, HEIGHT, WIDTH_CELLS, CH), 1.0, 6.0, ((0, 4), (1, 2), (3, 2))),
        "expanded": gaussian(part_keys[3], (FRAMES, HEIGHT, WIDTH_CELLS, 2, FF), 1.0, 6.0, ((0, 4), (1, 2), (4, 2))),
        "spatial_weight": jnp.clip(jax.random.uniform(key_of[4], (3, 3, 2, FF), jnp.float32, -0.6, 0.6) * block_scale(key_of[4], (3, 3, 2, FF), ((3, 2),), -0.4, 0.0), -0.6, 0.6),
        "temporal_weight": jnp.clip(jax.random.uniform(key_of[5], (3, 2, FF), jnp.float32, -1.0, 1.0) * block_scale(key_of[5], (3, 2, FF), ((2, 2),), -0.4, 0.0), -1.0, 1.0),
    }


def conv_plane(plane, spatial_weight):
    row_count = plane.shape[0]
    col_count = plane.shape[1]
    padded = jnp.pad(plane, ((1, 1), (1, 1), (0, 0), (0, 0)))
    summed = jnp.zeros(plane.shape, jnp.float32)
    for row_tap in range(3):
        for col_tap in range(3):
            summed = summed + padded[row_tap:row_tap + row_count, col_tap:col_tap + col_count].astype(jnp.float32) * spatial_weight[row_tap, col_tap]
    return summed.astype(jnp.bfloat16)


def reference(query_proj, key_proj, value_proj, expanded, spatial_weight, temporal_weight):
    tokens_frame = HEIGHT * WIDTH_CELLS
    key_relu = jnp.maximum(key_proj, 0).reshape(FRAMES, tokens_frame, HEADS, HEAD_DIM).astype(jnp.float32)
    value_all = value_proj.reshape(FRAMES, tokens_frame, HEADS, HEAD_DIM).astype(jnp.float32)
    frame_state = jnp.einsum('fthd,fthe->fdhe', key_relu, value_all, precision=lax.Precision.HIGHEST)
    frame_keys = jnp.sum(key_relu, axis=1)
    span_state = frame_state.reshape(N_TM, FR_DEV, HEAD_DIM, HEADS, HEAD_DIM).sum(axis=1)
    span_keys = frame_keys.reshape(N_TM, FR_DEV, HEADS, HEAD_DIM).sum(axis=1)
    state_prefix = jnp.cumsum(span_state, axis=0)
    keys_prefix = jnp.cumsum(span_keys, axis=0)
    query_relu = jnp.maximum(query_proj, 0).reshape(N_TM, FR_DEV * tokens_frame, HEADS, HEAD_DIM).astype(jnp.float32)
    numerator = jnp.einsum('cthd,cdhe->cthe', query_relu, state_prefix, precision=lax.Precision.HIGHEST)
    denominator = jnp.einsum('cthd,chd->cth', query_relu, keys_prefix, precision=lax.Precision.HIGHEST) + 1.0
    attended = (numerator / denominator[..., None]).reshape(FRAMES, HEIGHT, WIDTH_CELLS, CH).astype(jnp.bfloat16)

    def spatial_frame(plane):
        return conv_plane(plane, spatial_weight)

    spatial = lax.map(spatial_frame, expanded)
    padded_time = jnp.concatenate([jnp.zeros((2,) + spatial.shape[1:], jnp.bfloat16), spatial], axis=0)

    def temporal_frame(frame_index):
        window = lax.dynamic_slice_in_dim(padded_time, frame_index, 3, 0).astype(jnp.float32)
        mixed = window[0] * temporal_weight[0] + window[1] * temporal_weight[1] + window[2] * temporal_weight[2]
        return (mixed[..., 0, :] * jax.nn.silu(mixed[..., 1, :])).astype(jnp.bfloat16)

    gated_hidden = lax.map(temporal_frame, jnp.arange(FRAMES, dtype=jnp.int32))
    return attended, gated_hidden
```

```python
import functools

import jax
import jax.numpy as jnp
from jax import lax
from jax.experimental import pallas as pl
from jax.experimental.pallas import tpu as pltpu
from jax.sharding import PartitionSpec as P

HEAD_DIM = 32
LANES = 128
CHUNK = 3
ST = HEAD_DIM + 8
MESH = pl.DeviceIdType.MESH
F32 = jnp.float32
BF16 = jnp.bfloat16


def kernel(
    plan, q_ref, k_ref, v_ref, x_ref, sw_ref, tw_ref, att_ref, out_ref,
    spat, recv, outs, hsend, hrecv, state, rs_buf, prefix, pre_in, full,
    h_ss, h_rs, m_ss, m_rs, o_ss, o_rs, rs_ss, rs_rs, ag_ss, ag_rs, ch_ss, ch_rs,
):
    n_tm, n_sp, order, a_list, b_list = plan
    frames = x_ref.shape[1]
    cols = hsend.shape[2] // frames
    rows = x_ref.shape[2] // cols
    c = lax.axis_index("tm")
    s = lax.axis_index("space")
    has_prev, has_next = c > 0, c < n_tm - 1
    has_up, has_down = s > 0, s < n_sp - 1
    width = CHUNK * LANES

    def lanes(chunk):
        return pl.ds(chunk * width, width)

    def remote(src, dst, ss, rs, **where):
        return pltpu.make_async_remote_copy(
            src_ref=src, dst_ref=dst, send_sem=ss, recv_sem=rs,
            device_id=where, device_id_type=MESH,
        )

    def when(cond):
        return pl.when(cond)

    up_id, down_id = jnp.maximum(s - 1, 0), jnp.minimum(s + 1, n_sp - 1)
    prev_id, next_id = jnp.maximum(c - 1, 0), jnp.minimum(c + 1, n_tm - 1)

    barrier = pltpu.get_barrier_semaphore()
    for off in range(1, n_sp):
        pl.semaphore_signal(barrier, inc=1, device_id={"space": lax.rem(s + off, n_sp)}, device_id_type=MESH)

    @when(has_prev)
    def _():
        pl.semaphore_signal(barrier, inc=1, device_id={"tm": prev_id}, device_id_type=MESH)

    @when(has_next)
    def _():
        pl.semaphore_signal(barrier, inc=1, device_id={"tm": next_id}, device_id_type=MESH)

    n_tiles = x_ref.shape[3] // LANES

    def edges(t, _):
        at = pl.ds(pl.multiple_of(t * LANES, LANES), LANES)
        for vg in range(2):
            top = [x_ref[vg, f, 0 : 2 * cols, at].astype(F32)[:cols] for f in range(frames)]
            low = [x_ref[vg, f, (rows - 2) * cols : rows * cols, at].astype(F32)[cols:] for f in range(frames)]
            hsend[0, vg, :, at] = jnp.concatenate(top, axis=0).astype(BF16)
            hsend[1, vg, :, at] = jnp.concatenate(low, axis=0).astype(BF16)
        return 0

    lax.fori_loop(0, n_tiles, edges, 0)

    @when(jnp.logical_not(has_up))
    def _():
        hrecv[0] = jnp.zeros(hrecv.shape[1:], BF16)

    @when(jnp.logical_not(has_down))
    def _():
        hrecv[1] = jnp.zeros(hrecv.shape[1:], BF16)

    pl.semaphore_wait(barrier, n_sp - 1 + jnp.minimum(c, 1) + jnp.minimum(n_tm - 1 - c, 1))

    def halo(chunk, way):
        return remote(
            hsend.at[way, :, :, lanes(chunk)], hrecv.at[1 - way, :, :, lanes(chunk)],
            h_ss.at[way, chunk], h_rs.at[1 - way, chunk], space=up_id if way == 0 else down_id,
        )

    def halo_in(chunk, side):
        return remote(
            hsend.at[side, :, :, lanes(chunk)], hrecv.at[side, :, :, lanes(chunk)],
            h_ss.at[side, chunk], h_rs.at[side, chunk], space=up_id if side == 0 else down_id,
        )

    for chunk in order:
        for way, cond in ((0, has_up), (1, has_down)):
            when(cond)(lambda chunk=chunk, way=way: halo(chunk, way).start())

    channels = q_ref.shape[-1]
    heads_tiles = -(-channels // LANES)
    tokens = q_ref.shape[0]
    row_id = lax.broadcasted_iota(jnp.int32, (LANES, LANES), 0) // HEAD_DIM
    col_id = lax.broadcasted_iota(jnp.int32, (LANES, LANES), 1) // HEAD_DIM
    same = row_id == col_id

    def tile_of(ref, t):
        lo, hi = t * LANES, min(channels, (t + 1) * LANES)
        part = ref[:, lo:hi].astype(F32)
        if hi - lo < LANES:
            part = jnp.concatenate([part, jnp.zeros((tokens, LANES - hi + lo), F32)], axis=1)
        return part

    for t in range(heads_tiles):
        key = jnp.maximum(tile_of(k_ref, t), 0.0)
        kv = lax.dot_general(
            key.T.astype(BF16), tile_of(v_ref, t).astype(BF16),
            (((1,), (0,)), ((), ())), preferred_element_type=F32,
        )
        kv = jnp.where(same, kv, 0.0)
        small = kv[:HEAD_DIM]
        for j in range(1, LANES // HEAD_DIM):
            small = small + kv[j * HEAD_DIM : (j + 1) * HEAD_DIM]
        state[t, :HEAD_DIM] = small
        state[t, HEAD_DIM:] = jnp.broadcast_to(jnp.sum(key, axis=0, keepdims=True), (ST - HEAD_DIM, LANES))
    for t in range(heads_tiles, state.shape[0]):
        state[t] = jnp.zeros((ST, LANES), F32)

    per = state.shape[0] // n_sp

    def share(dev):
        return pl.ds(dev * per, per)

    def scatter(off):
        peer = lax.rem(s + off, n_sp)
        return remote(state.at[share(peer)], rs_buf.at[off - 1], rs_ss.at[off - 1], rs_rs.at[off - 1], space=peer)

    def gather(off):
        peer = lax.rem(s + off, n_sp)
        return remote(prefix, full.at[off - 1], ag_ss.at[off - 1], ag_rs.at[off - 1], space=peer)

    for off in range(1, n_sp):
        scatter(off).start()

    def chain():
        return remote(prefix, pre_in, ch_ss, ch_rs, tm=next_id)

    def hop():
        total = state[share(s)]
        for off in range(1, n_sp):
            total = total + rs_buf[off - 1]

        @when(has_prev)
        def _():
            chain().wait_recv()
            prefix[...] = total + pre_in[...]

        @when(jnp.logical_not(has_prev))
        def _():
            prefix[...] = total

        when(has_next)(lambda: chain().start())
        for off in range(1, n_sp):
            gather(off).start()

    col = lax.broadcasted_iota(jnp.int32, (cols, LANES), 0)

    def conv(chunk):
        def tile(t, _):
            at = pl.ds(pl.multiple_of(chunk * width + t * LANES, LANES), LANES)
            for vg in range(2):
                taps = []
                for a in range(3):
                    for b in range(3):
                        w = jnp.broadcast_to(sw_ref[a, b, vg : vg + 1, at], (cols, LANES))
                        if b == 0:
                            w = jnp.where(col == 0, 0.0, w)
                        if b == 2:
                            w = jnp.where(col == cols - 1, 0.0, w)
                        taps.append(w[None])
                above = hrecv[0, vg, :, at].astype(F32).reshape(frames, 1, cols, LANES)
                below = hrecv[1, vg, :, at].astype(F32).reshape(frames, 1, cols, LANES)
                for f in range(frames):
                    body = x_ref[vg, f, :, at].astype(F32).reshape(rows, cols, LANES)
                    ext = jnp.concatenate([above[f], body, below[f]], axis=0)
                    moved = [pltpu.roll(ext, 1, 1), ext, pltpu.roll(ext, cols - 1, 1)]
                    total = None
                    for a in range(3):
                        for b in range(3):
                            term = moved[b][a : a + rows] * taps[3 * a + b]
                            total = term if total is None else total + term
                    spat[vg, f, :, at] = total.reshape(rows * cols, LANES).astype(BF16)
            return 0

        lax.fori_loop(0, CHUNK, tile, 0)

    def gate(chunk, before, now, into):
        def tile(t, _):
            at = pl.ds(pl.multiple_of(chunk * width + t * LANES, LANES), LANES)
            mixed = []
            for vg in range(2):
                w = [tw_ref[j, vg : vg + 1, at] for j in range(3)]
                line = [now[vg, f, :, at].astype(F32) for f in range(frames)]
                if before is not None:
                    line = [before[vg, f, :, at].astype(F32) for f in (frames - 2, frames - 1)] + line
                    mixed.append([line[f] * w[0] + line[f + 1] * w[1] + line[f + 2] * w[2] for f in range(frames)])
                else:
                    got = []
                    for f in range(frames):
                        m = line[f] * w[2]
                        if f >= 1:
                            m = line[f - 1] * w[1] + m
                        if f >= 2:
                            m = line[f - 2] * w[0] + m
                        got.append(m)
                    mixed.append(got)
            for f in range(frames):
                v, g = mixed[0][f], mixed[1][f]
                into[f, :, at] = (v * (g / (1.0 + jnp.exp(-g)))).astype(BF16)
            return 0

        lax.fori_loop(0, CHUNK, tile, 0)

    def ahead(chunk):
        part = (slice(None), slice(None), slice(None), lanes(chunk))
        return remote(spat.at[part], recv.at[part], m_ss.at[chunk], m_rs.at[chunk], tm=next_id)

    def back(chunk):
        part = (slice(None), slice(None), slice(None), lanes(chunk))
        return remote(spat.at[part], recv.at[part], m_ss.at[chunk], m_rs.at[chunk], tm=prev_id)

    def give(chunk):
        part = (slice(None), slice(None), lanes(chunk))
        return remote(outs.at[part], out_ref.at[part], o_ss.at[chunk], o_rs.at[chunk], tm=next_id)

    def finish_attention():
        for off in range(1, n_sp):
            gather(off).wait_recv()
        for t in range(heads_tiles):
            owner, local = t // per, t % per
            tile = prefix[local]
            for off in range(1, n_sp):
                tile = jnp.where(lax.rem(s + n_sp - off, n_sp) == owner, full[off - 1, local], tile)
            big = jnp.concatenate([tile[:HEAD_DIM]] * (LANES // HEAD_DIM), axis=0)
            keys = jnp.broadcast_to(tile[HEAD_DIM : HEAD_DIM + 1], (LANES, LANES)).T
            both = jnp.concatenate([jnp.where(same, big, 0.0), jnp.where(same, keys, 0.0)], axis=1)
            high = both.astype(BF16)
            low = (both - high.astype(F32)).astype(BF16)
            query = jnp.maximum(tile_of(q_ref, t), 0.0).astype(BF16)
            got = jnp.dot(query, high, preferred_element_type=F32) + jnp.dot(query, low, preferred_element_type=F32)
            value = (got[:, :LANES] / (got[:, LANES:] + 1.0)).astype(BF16)
            lo, hi = t * LANES, min(channels, (t + 1) * LANES)
            att_ref[:, lo:hi] = value[:, : hi - lo]

    sent_back = 0
    for place, chunk in enumerate(order):
        for side, cond in ((0, has_up), (1, has_down)):
            when(cond)(lambda chunk=chunk, side=side: halo_in(chunk, side).wait_recv())
        conv(chunk)
        if chunk in a_list:
            when(has_next)(lambda chunk=chunk: ahead(chunk).start())
        elif sent_back < 2:
            when(has_prev)(lambda chunk=chunk: back(chunk).start())
            sent_back += 1
        if place == 0:
            for off in range(1, n_sp):
                scatter(off).wait_recv()
            when(c == 0)(hop)

    @when(jnp.logical_not(has_prev))
    def _():
        for chunk in a_list:
            gate(chunk, None, spat, out_ref)

    for i, chunk in enumerate(b_list):
        @when(jnp.logical_not(has_prev))
        def _():
            gate(chunk, None, spat, out_ref)

        @when(has_next)
        def _():
            back(chunk).wait_recv()
            gate(chunk, spat, recv, outs)
            give(chunk).start()

        @when(has_prev)
        def _():
            back(chunk).wait_send()
            if i + 2 < len(b_list):
                back(b_list[i + 2]).start()

        last = i == max(0, len(b_list) - 2)
        if last:
            when(jnp.logical_and(has_prev, c >= i + 1))(hop)
            finish_attention()
        elif i < len(b_list) - 2:
            when(c == i + 1)(hop)
        if i >= 2 and i - 2 < len(a_list) - 1 and i < len(b_list) - 1:
            @when(has_prev)
            def _():
                ahead(a_list[i - 2]).wait_recv()
                gate(a_list[i - 2], recv, spat, out_ref)

    done = len([i for i in range(len(b_list)) if i >= 2 and i - 2 < len(a_list) - 1 and i < len(b_list) - 1])

    @when(has_prev)
    def _():
        for chunk in a_list[done:]:
            ahead(chunk).wait_recv()
            gate(chunk, recv, spat, out_ref)
        for chunk in b_list:
            give(chunk).wait_recv()

    @when(has_next)
    def _():
        for chunk in a_list:
            ahead(chunk).wait_send()
        for chunk in b_list:
            give(chunk).wait_send()
        chain().wait_send()

    for off in range(1, n_sp):
        scatter(off).wait_send()
        gather(off).wait_send()
    for chunk in order:
        for way, cond in ((0, has_up), (1, has_down)):
            when(cond)(lambda chunk=chunk, way=way: halo(chunk, way).wait_send())


def plan_of(n_tm, n_sp, chunks):
    n_a = max(1, round(chunks / 3))
    a_list = list(range(n_a))
    b_list = list(range(n_a, chunks))
    order = []
    for i in range(max(len(a_list), len(b_list))):
        order += b_list[i : i + 1] + a_list[i : i + 1]
    return n_tm, n_sp, order, a_list, b_list


def on_device(query_proj, key_proj, value_proj, expanded, spatial_weight, temporal_weight):
    n_tm, n_sp = lax.axis_size("tm"), lax.axis_size("space")
    frames, rows, cols, channels = query_proj.shape
    hidden = expanded.shape[-1]
    chunks = -(-hidden // (CHUNK * LANES))
    padded = chunks * CHUNK * LANES
    extra = padded - hidden
    tokens = frames * rows * cols
    x = jnp.pad(expanded.transpose(3, 0, 1, 2, 4), ((0, 0),) * 4 + ((0, extra),))
    x = x.reshape(2, frames, rows * cols, padded)
    sw = jnp.pad(spatial_weight, ((0, 0),) * 3 + ((0, extra),))
    tw = jnp.pad(temporal_weight, ((0, 0),) * 2 + ((0, extra),))
    per = -(-(-(-channels // LANES)) // n_sp)
    dma = pltpu.SemaphoreType.DMA
    vmem = pl.BlockSpec(memory_space=pltpu.VMEM)
    att, out = pl.pallas_call(
        functools.partial(kernel, plan_of(n_tm, n_sp, chunks)),
        out_shape=(
            jax.ShapeDtypeStruct((tokens, channels), BF16),
            jax.ShapeDtypeStruct((frames, rows * cols, padded), BF16),
        ),
        in_specs=[vmem] * 6,
        out_specs=(vmem, vmem),
        scratch_shapes=[
            pltpu.VMEM((2, frames, rows * cols, padded), BF16),
            pltpu.VMEM((2, frames, rows * cols, padded), BF16),
            pltpu.VMEM((frames, rows * cols, padded), BF16),
            pltpu.VMEM((2, 2, frames * cols, padded), BF16),
            pltpu.VMEM((2, 2, frames * cols, padded), BF16),
            pltpu.VMEM((per * n_sp, ST, LANES), F32),
            pltpu.VMEM((n_sp - 1, per, ST, LANES), F32),
            pltpu.VMEM((per, ST, LANES), F32),
            pltpu.VMEM((per, ST, LANES), F32),
            pltpu.VMEM((n_sp - 1, per, ST, LANES), F32),
            dma((2, chunks)), dma((2, chunks)),
            dma((chunks,)), dma((chunks,)),
            dma((chunks,)), dma((chunks,)),
            dma((n_sp - 1,)), dma((n_sp - 1,)),
            dma((n_sp - 1,)), dma((n_sp - 1,)),
            dma, dma,
        ],
        compiler_params=pltpu.CompilerParams(
            collective_id=0, has_side_effects=True, vmem_limit_bytes=40 * 1024 * 1024
        ),
    )(
        query_proj.reshape(tokens, channels),
        key_proj.reshape(tokens, channels),
        value_proj.reshape(tokens, channels),
        x, sw, tw,
    )
    attended = att.reshape(frames, rows, cols, channels)
    gated = out.reshape(frames, rows, cols, padded)[..., :hidden]
    return attended, gated


def solution(mesh):
    token = P(("groups", "tm"), "space", None, "mp")
    return jax.shard_map(
        on_device,
        mesh=mesh,
        in_specs=(
            token, token, token,
            P(("groups", "tm"), "space", None, None, "mp"),
            P(None, None, None, "mp"),
            P(None, None, "mp"),
        ),
        out_specs=(token, token),
        check_vma=False,
    )
```

```python
import functools

import jax
import jax.numpy as jnp
from jax import lax
from jax.experimental import pallas as pl
from jax.experimental.pallas import tpu as pltpu
from jax.sharding import PartitionSpec as P

HEAD_DIM = 32
LANES = 128
EARLY = 4
LATE = 3
CHUNK = 4
A_SHARE = 1 / 3
B_CHUNK = 4
AHEAD = 4
ST = HEAD_DIM + 8
MESH = pl.DeviceIdType.MESH
F32 = jnp.float32
BF16 = jnp.bfloat16


def kernel(
    plan, q_ref, k_ref, v_ref, x_ref, sw_ref, tw_ref, att_ref, out_ref,
    spat, recv, outs, hsend, hrecv, state, rs_buf, prefix, pre_in, full,
    h_ss, h_rs, m_ss, m_rs, o_ss, o_rs, rs_ss, rs_rs, ag_ss, ag_rs, ch_ss, ch_rs,
):
    n_tm, n_sp, order, a_list, b_list, spans = plan
    frames = x_ref.shape[1]
    cols = hsend.shape[2] // frames
    rows = x_ref.shape[2] // cols
    c = lax.axis_index("tm")
    s = lax.axis_index("space")
    has_prev, has_next = c > 0, c < n_tm - 1
    has_up, has_down = s > 0, s < n_sp - 1

    def lanes(chunk):
        return pl.ds(spans[chunk][0] * LANES, spans[chunk][1] * LANES)

    def remote(src, dst, ss, rs, **where):
        return pltpu.make_async_remote_copy(
            src_ref=src, dst_ref=dst, send_sem=ss, recv_sem=rs,
            device_id=where, device_id_type=MESH,
        )

    def when(cond):
        return pl.when(cond)

    up_id, down_id = jnp.maximum(s - 1, 0), jnp.minimum(s + 1, n_sp - 1)
    prev_id, next_id = jnp.maximum(c - 1, 0), jnp.minimum(c + 1, n_tm - 1)

    barrier = pltpu.get_barrier_semaphore()
    for off in range(1, n_sp):
        pl.semaphore_signal(barrier, inc=1, device_id={"space": lax.rem(s + off, n_sp)}, device_id_type=MESH)

    @when(has_prev)
    def _():
        pl.semaphore_signal(barrier, inc=1, device_id={"tm": prev_id}, device_id_type=MESH)

    @when(has_next)
    def _():
        pl.semaphore_signal(barrier, inc=1, device_id={"tm": next_id}, device_id_type=MESH)


    def edges(t, _):
        at = pl.ds(pl.multiple_of(t * LANES, LANES), LANES)
        for vg in range(2):
            top = [x_ref[vg, f, 0 : 2 * cols, at].astype(F32)[:cols] for f in range(frames)]
            low = [x_ref[vg, f, (rows - 2) * cols : rows * cols, at].astype(F32)[cols:] for f in range(frames)]
            hsend[0, vg, :, at] = jnp.concatenate(top, axis=0).astype(BF16)
            hsend[1, vg, :, at] = jnp.concatenate(low, axis=0).astype(BF16)
        return 0

    def edges_of(chunk):
        lax.fori_loop(spans[chunk][0], sum(spans[chunk]), edges, 0)

    for chunk in order[:EARLY]:
        edges_of(chunk)

    @when(jnp.logical_not(has_up))
    def _():
        hrecv[0] = jnp.zeros(hrecv.shape[1:], BF16)

    @when(jnp.logical_not(has_down))
    def _():
        hrecv[1] = jnp.zeros(hrecv.shape[1:], BF16)

    pl.semaphore_wait(barrier, n_sp - 1 + jnp.minimum(c, 1) + jnp.minimum(n_tm - 1 - c, 1))

    def halo(chunk, way):
        return remote(
            hsend.at[way, :, :, lanes(chunk)], hrecv.at[1 - way, :, :, lanes(chunk)],
            h_ss.at[way, chunk], h_rs.at[1 - way, chunk], space=up_id if way == 0 else down_id,
        )

    def halo_in(chunk, side):
        return remote(
            hsend.at[side, :, :, lanes(chunk)], hrecv.at[side, :, :, lanes(chunk)],
            h_ss.at[side, chunk], h_rs.at[side, chunk], space=up_id if side == 0 else down_id,
        )

    def send_edges(chunk):
        for way, cond in ((0, has_up), (1, has_down)):
            when(cond)(lambda way=way: halo(chunk, way).start())

    for chunk in order[:EARLY]:
        send_edges(chunk)
    for chunk in order[EARLY:]:
        edges_of(chunk)
        send_edges(chunk)

    channels = q_ref.shape[-1]
    heads_tiles = -(-channels // LANES)
    tokens = q_ref.shape[0]
    row_id = lax.broadcasted_iota(jnp.int32, (LANES, LANES), 0) // HEAD_DIM
    col_id = lax.broadcasted_iota(jnp.int32, (LANES, LANES), 1) // HEAD_DIM
    same = row_id == col_id

    def tile_of(ref, t):
        lo, hi = t * LANES, min(channels, (t + 1) * LANES)
        part = ref[:, lo:hi].astype(F32)
        if hi - lo < LANES:
            part = jnp.concatenate([part, jnp.zeros((tokens, LANES - hi + lo), F32)], axis=1)
        return part

    def local_state():
        for t in range(heads_tiles):
            key = jnp.maximum(tile_of(k_ref, t), 0.0)
            kv = lax.dot_general(
                key.T.astype(BF16), tile_of(v_ref, t).astype(BF16),
                (((1,), (0,)), ((), ())), preferred_element_type=F32,
            )
            kv = jnp.where(same, kv, 0.0)
            small = kv[:HEAD_DIM]
            for j in range(1, LANES // HEAD_DIM):
                small = small + kv[j * HEAD_DIM : (j + 1) * HEAD_DIM]
            state[t, :HEAD_DIM] = small
            state[t, HEAD_DIM:] = jnp.broadcast_to(jnp.sum(key, axis=0, keepdims=True), (ST - HEAD_DIM, LANES))
        for t in range(heads_tiles, state.shape[0]):
            state[t] = jnp.zeros((ST, LANES), F32)

    per = state.shape[0] // n_sp

    def share(dev):
        return pl.ds(dev * per, per)

    def scatter(off):
        peer = lax.rem(s + off, n_sp)
        return remote(state.at[share(peer)], rs_buf.at[off - 1], rs_ss.at[off - 1], rs_rs.at[off - 1], space=peer)

    def gather(off):
        peer = lax.rem(s + off, n_sp)
        return remote(prefix, full.at[off - 1], ag_ss.at[off - 1], ag_rs.at[off - 1], space=peer)


    def chain():
        return remote(prefix, pre_in, ch_ss, ch_rs, tm=next_id)

    def hop():
        total = state[share(s)]
        for off in range(1, n_sp):
            total = total + rs_buf[off - 1]

        @when(has_prev)
        def _():
            chain().wait_recv()
            prefix[...] = total + pre_in[...]

        @when(jnp.logical_not(has_prev))
        def _():
            prefix[...] = total

        when(has_next)(lambda: chain().start())
        for off in range(1, n_sp):
            gather(off).start()

    col = lax.broadcasted_iota(jnp.int32, (cols, LANES), 0)

    def conv(chunk):
        def tile(t, _):
            at = pl.ds(pl.multiple_of((spans[chunk][0] + t) * LANES, LANES), LANES)
            for vg in range(2):
                taps = []
                for a in range(3):
                    for b in range(3):
                        w = jnp.broadcast_to(sw_ref[a, b, vg : vg + 1, at], (cols, LANES))
                        if b == 0:
                            w = jnp.where(col == 0, 0.0, w)
                        if b == 2:
                            w = jnp.where(col == cols - 1, 0.0, w)
                        taps.append(w[None])
                above = hrecv[0, vg, :, at].astype(F32).reshape(frames, 1, cols, LANES)
                below = hrecv[1, vg, :, at].astype(F32).reshape(frames, 1, cols, LANES)
                for f in range(frames):
                    body = x_ref[vg, f, :, at].astype(F32).reshape(rows, cols, LANES)
                    ext = jnp.concatenate([above[f], body, below[f]], axis=0)
                    moved = [pltpu.roll(ext, 1, 1), ext, pltpu.roll(ext, cols - 1, 1)]
                    total = None
                    for a in range(3):
                        for b in range(3):
                            term = moved[b][a : a + rows] * taps[3 * a + b]
                            total = term if total is None else total + term
                    spat[vg, f, :, at] = total.reshape(rows * cols, LANES).astype(BF16)
            return 0

        lax.fori_loop(0, spans[chunk][1], tile, 0)

    def gate(chunk, before, now, into):
        def tile(t, _):
            at = pl.ds(pl.multiple_of((spans[chunk][0] + t) * LANES, LANES), LANES)
            mixed = []
            for vg in range(2):
                w = [tw_ref[j, vg : vg + 1, at] for j in range(3)]
                line = [now[vg, f, :, at].astype(F32) for f in range(frames)]
                if before is not None:
                    line = [before[vg, f, :, at].astype(F32) for f in (frames - 2, frames - 1)] + line
                    mixed.append([line[f] * w[0] + line[f + 1] * w[1] + line[f + 2] * w[2] for f in range(frames)])
                else:
                    got = []
                    for f in range(frames):
                        m = line[f] * w[2]
                        if f >= 1:
                            m = line[f - 1] * w[1] + m
                        if f >= 2:
                            m = line[f - 2] * w[0] + m
                        got.append(m)
                    mixed.append(got)
            for f in range(frames):
                v, g = mixed[0][f], mixed[1][f]
                into[f, :, at] = (v * (g / (1.0 + jnp.exp(-g)))).astype(BF16)
            return 0

        lax.fori_loop(0, spans[chunk][1], tile, 0)

    def ahead(chunk):
        part = (slice(None), slice(None), slice(None), lanes(chunk))
        return remote(spat.at[part], recv.at[part], m_ss.at[chunk], m_rs.at[chunk], tm=next_id)

    def back(chunk):
        part = (slice(None), slice(None), slice(None), lanes(chunk))
        return remote(spat.at[part], recv.at[part], m_ss.at[chunk], m_rs.at[chunk], tm=prev_id)

    def give(chunk):
        part = (slice(None), slice(None), lanes(chunk))
        return remote(outs.at[part], out_ref.at[part], o_ss.at[chunk], o_rs.at[chunk], tm=next_id)

    def finish_attention():
        for off in range(1, n_sp):
            gather(off).wait_recv()
        for t in range(heads_tiles):
            owner, local = t // per, t % per
            tile = prefix[local]
            for off in range(1, n_sp):
                tile = jnp.where(lax.rem(s + n_sp - off, n_sp) == owner, full[off - 1, local], tile)
            big = jnp.concatenate([tile[:HEAD_DIM]] * (LANES // HEAD_DIM), axis=0)
            keys = jnp.broadcast_to(tile[HEAD_DIM : HEAD_DIM + 1], (LANES, LANES)).T
            both = jnp.concatenate([jnp.where(same, big, 0.0), jnp.where(same, keys, 0.0)], axis=1)
            high = both.astype(BF16)
            low = (both - high.astype(F32)).astype(BF16)
            query = jnp.maximum(tile_of(q_ref, t), 0.0).astype(BF16)
            got = jnp.dot(query, high, preferred_element_type=F32) + jnp.dot(query, low, preferred_element_type=F32)
            value = (got[:, :LANES] / (got[:, LANES:] + 1.0)).astype(BF16)
            lo, hi = t * LANES, min(channels, (t + 1) * LANES)
            att_ref[:, lo:hi] = value[:, : hi - lo]

    sent_back = 0
    for place, chunk in enumerate(order):
        for side, cond in ((0, has_up), (1, has_down)):
            when(cond)(lambda chunk=chunk, side=side: halo_in(chunk, side).wait_recv())
        conv(chunk)
        if chunk in a_list[:2]:
            when(has_next)(lambda chunk=chunk: ahead(chunk).start())
        elif chunk in b_list and sent_back < AHEAD:
            when(has_prev)(lambda chunk=chunk: back(chunk).start())
            sent_back += 1
        if place == min(LATE, len(order) - 1):
            local_state()
            for off in range(1, n_sp):
                scatter(off).start()
        if place == min(LATE + 1, len(order) - 1):
            for off in range(1, n_sp):
                scatter(off).wait_recv()
            when(c == 0)(hop)

    @when(jnp.logical_not(has_prev))
    def _():
        for chunk in a_list:
            gate(chunk, None, spat, out_ref)

    for chunk in a_list[len(b_list) + 1 :]:
        when(has_next)(lambda chunk=chunk: ahead(chunk).start())
    finish = max(1, len(b_list) - 2)
    for i, chunk in enumerate(b_list):
        @when(jnp.logical_not(has_prev))
        def _():
            gate(chunk, None, spat, out_ref)

        @when(has_next)
        def _():
            back(chunk).wait_recv()
            gate(chunk, spat, recv, outs)
            give(chunk).start()

        @when(has_prev)
        def _():
            back(chunk).wait_send()
            if i + AHEAD < len(b_list):
                back(b_list[i + AHEAD]).start()

        if 2 <= i + 1 < len(a_list):
            when(has_next)(lambda i=i: ahead(a_list[i + 1]).start())
        if i == finish:
            when(jnp.logical_and(has_prev, c >= i))(hop)
            finish_attention()
        elif 1 <= i < finish:
            when(c == i)(hop)
        if 2 <= i < len(b_list) - 1 and i - 2 < len(a_list):
            @when(has_prev)
            def _():
                ahead(a_list[i - 2]).wait_recv()
                gate(a_list[i - 2], recv, spat, out_ref)

    done = max(0, min(len(a_list), len(b_list) - 3))

    @when(has_prev)
    def _():
        for chunk in a_list[done:]:
            ahead(chunk).wait_recv()
            gate(chunk, recv, spat, out_ref)
        for chunk in b_list:
            give(chunk).wait_recv()

    @when(has_next)
    def _():
        for chunk in a_list:
            ahead(chunk).wait_send()
        for chunk in b_list:
            give(chunk).wait_send()
        chain().wait_send()

    for off in range(1, n_sp):
        scatter(off).wait_send()
        gather(off).wait_send()
    for chunk in order:
        for way, cond in ((0, has_up), (1, has_down)):
            when(cond)(lambda chunk=chunk, way=way: halo(chunk, way).wait_send())


def cut(total, most):
    count = -(-total // most)
    return [total // count + (1 if i < total % count else 0) for i in range(count)]


def plan_of(n_tm, n_sp, tiles):
    forward = max(1, round(tiles * A_SHARE))
    a_sizes = [1] + cut(forward - 1, CHUNK) if forward > 1 else [forward]
    rest = tiles - forward
    b_sizes = [1, 2] + cut(rest - 6, B_CHUNK) + [2, 1] if rest >= 8 else [1] * rest
    spans, at = [], 0
    for size in a_sizes + b_sizes:
        spans.append((at, size))
        at += size
    a_list = list(range(len(a_sizes)))
    b_list = list(range(len(a_sizes), len(spans)))
    order = []
    for i in range(max(len(a_list), len(b_list))):
        order += b_list[i : i + 1] + a_list[i : i + 1]
    return n_tm, n_sp, order, a_list, b_list, spans


def on_device(query_proj, key_proj, value_proj, expanded, spatial_weight, temporal_weight):
    n_tm, n_sp = lax.axis_size("tm"), lax.axis_size("space")
    frames, rows, cols, channels = query_proj.shape
    hidden = expanded.shape[-1]
    tiles = -(-hidden // LANES)
    padded = tiles * LANES
    extra = padded - hidden
    tokens = frames * rows * cols
    x = jnp.pad(expanded.transpose(3, 0, 1, 2, 4), ((0, 0),) * 4 + ((0, extra),))
    x = x.reshape(2, frames, rows * cols, padded)
    sw = jnp.pad(spatial_weight, ((0, 0),) * 3 + ((0, extra),))
    tw = jnp.pad(temporal_weight, ((0, 0),) * 2 + ((0, extra),))
    per = -(-(-(-channels // LANES)) // n_sp)
    plan = plan_of(n_tm, n_sp, tiles)
    chunks = len(plan[-1])
    dma = pltpu.SemaphoreType.DMA
    vmem = pl.BlockSpec(memory_space=pltpu.VMEM)
    att, out = pl.pallas_call(
        functools.partial(kernel, plan),
        out_shape=(
            jax.ShapeDtypeStruct((tokens, channels), BF16),
            jax.ShapeDtypeStruct((frames, rows * cols, padded), BF16),
        ),
        in_specs=[vmem] * 6,
        out_specs=(vmem, vmem),
        scratch_shapes=[
            pltpu.VMEM((2, frames, rows * cols, padded), BF16),
            pltpu.VMEM((2, frames, rows * cols, padded), BF16),
            pltpu.VMEM((frames, rows * cols, padded), BF16),
            pltpu.VMEM((2, 2, frames * cols, padded), BF16),
            pltpu.VMEM((2, 2, frames * cols, padded), BF16),
            pltpu.VMEM((per * n_sp, ST, LANES), F32),
            pltpu.VMEM((n_sp - 1, per, ST, LANES), F32),
            pltpu.VMEM((per, ST, LANES), F32),
            pltpu.VMEM((per, ST, LANES), F32),
            pltpu.VMEM((n_sp - 1, per, ST, LANES), F32),
            dma((2, chunks)), dma((2, chunks)),
            dma((chunks,)), dma((chunks,)),
            dma((chunks,)), dma((chunks,)),
            dma((n_sp - 1,)), dma((n_sp - 1,)),
            dma((n_sp - 1,)), dma((n_sp - 1,)),
            dma, dma,
        ],
        compiler_params=pltpu.CompilerParams(
            collective_id=0, has_side_effects=True, vmem_limit_bytes=40 * 1024 * 1024
        ),
    )(
        query_proj.reshape(tokens, channels),
        key_proj.reshape(tokens, channels),
        value_proj.reshape(tokens, channels),
        x, sw, tw,
    )
    attended = att.reshape(frames, rows, cols, channels)
    gated = out.reshape(frames, rows, cols, padded)[..., :hidden]
    return attended, gated


def solution(mesh):
    token = P(("groups", "tm"), "space", None, "mp")
    return jax.shard_map(
        on_device,
        mesh=mesh,
        in_specs=(
            token, token, token,
            P(("groups", "tm"), "space", None, None, "mp"),
            P(None, None, None, "mp"),
            P(None, None, "mp"),
        ),
        out_specs=(token, token),
        check_vma=False,
    )
```

```python
import functools

import jax
import jax.numpy as jnp
from jax import lax
from jax.experimental import pallas as pl
from jax.experimental.pallas import tpu as pltpu
from jax.sharding import PartitionSpec as P

HEAD_DIM = 32
LANES = 128
EARLY = 4
LATE = 3
CHUNK = 4
A_SHARE = 1 / 3
B_CHUNK = 4
AHEAD = 4
ST = HEAD_DIM + 8
MESH = pl.DeviceIdType.MESH
F32 = jnp.float32
BF16 = jnp.bfloat16


def kernel(
    plan, q_ref, k_ref, v_ref, x_ref, sw_ref, tw_ref, att_ref, out_ref,
    spat, recv, outs, hsend, hrecv, state, rs_buf, prefix, pre_in, full,
    h_ss, h_rs, m_ss, m_rs, o_ss, o_rs, rs_ss, rs_rs, ag_ss, ag_rs, ch_ss, ch_rs,
):
    n_tm, n_sp, order, a_list, b_list, spans = plan
    frames = x_ref.shape[1]
    cols = hsend.shape[2] // frames
    rows = x_ref.shape[2] // cols
    c = lax.axis_index("tm")
    s = lax.axis_index("space")
    has_prev, has_next = c > 0, c < n_tm - 1
    has_up, has_down = s > 0, s < n_sp - 1

    def lanes(chunk):
        return pl.ds(spans[chunk][0] * LANES, spans[chunk][1] * LANES)

    def remote(src, dst, ss, rs, **where):
        return pltpu.make_async_remote_copy(
            src_ref=src, dst_ref=dst, send_sem=ss, recv_sem=rs,
            device_id=where, device_id_type=MESH,
        )

    def when(cond):
        return pl.when(cond)

    up_id, down_id = jnp.maximum(s - 1, 0), jnp.minimum(s + 1, n_sp - 1)
    prev_id, next_id = jnp.maximum(c - 1, 0), jnp.minimum(c + 1, n_tm - 1)

    barrier = pltpu.get_barrier_semaphore()
    for off in range(1, n_sp):
        pl.semaphore_signal(barrier, inc=1, device_id={"space": lax.rem(s + off, n_sp)}, device_id_type=MESH)

    @when(has_prev)
    def _():
        pl.semaphore_signal(barrier, inc=1, device_id={"tm": prev_id}, device_id_type=MESH)

    @when(has_next)
    def _():
        pl.semaphore_signal(barrier, inc=1, device_id={"tm": next_id}, device_id_type=MESH)


    def edges(t, _):
        at = pl.ds(pl.multiple_of(t * LANES, LANES), LANES)
        for vg in range(2):
            top = [x_ref[vg, f, 0 : 2 * cols, at].astype(F32)[:cols] for f in range(frames)]
            low = [x_ref[vg, f, (rows - 2) * cols : rows * cols, at].astype(F32)[cols:] for f in range(frames)]
            hsend[0, vg, :, at] = jnp.concatenate(top, axis=0).astype(BF16)
            hsend[1, vg, :, at] = jnp.concatenate(low, axis=0).astype(BF16)
        return 0

    def edges_of(chunk):
        lax.fori_loop(spans[chunk][0], sum(spans[chunk]), edges, 0)

    for chunk in order[:EARLY]:
        edges_of(chunk)

    @when(jnp.logical_not(has_up))
    def _():
        hrecv[0] = jnp.zeros(hrecv.shape[1:], BF16)

    @when(jnp.logical_not(has_down))
    def _():
        hrecv[1] = jnp.zeros(hrecv.shape[1:], BF16)

    pl.semaphore_wait(barrier, n_sp - 1 + jnp.minimum(c, 1) + jnp.minimum(n_tm - 1 - c, 1))

    def halo(chunk, way):
        return remote(
            hsend.at[way, :, :, lanes(chunk)], hrecv.at[1 - way, :, :, lanes(chunk)],
            h_ss.at[way, chunk], h_rs.at[1 - way, chunk], space=up_id if way == 0 else down_id,
        )

    def halo_in(chunk, side):
        return remote(
            hsend.at[side, :, :, lanes(chunk)], hrecv.at[side, :, :, lanes(chunk)],
            h_ss.at[side, chunk], h_rs.at[side, chunk], space=up_id if side == 0 else down_id,
        )

    def send_edges(chunk):
        for way, cond in ((0, has_up), (1, has_down)):
            when(cond)(lambda way=way: halo(chunk, way).start())

    for chunk in order[:EARLY]:
        send_edges(chunk)
    for chunk in order[EARLY:]:
        edges_of(chunk)
        send_edges(chunk)

    channels = q_ref.shape[-1]
    heads_tiles = -(-channels // LANES)
    tokens = q_ref.shape[0]
    row_id = lax.broadcasted_iota(jnp.int32, (LANES, LANES), 0) // HEAD_DIM
    col_id = lax.broadcasted_iota(jnp.int32, (LANES, LANES), 1) // HEAD_DIM
    same = row_id == col_id

    def tile_of(ref, t):
        lo, hi = t * LANES, min(channels, (t + 1) * LANES)
        part = ref[:, lo:hi].astype(F32)
        if hi - lo < LANES:
            part = jnp.concatenate([part, jnp.zeros((tokens, LANES - hi + lo), F32)], axis=1)
        return part

    def local_state():
        for t in range(heads_tiles):
            key = jnp.maximum(tile_of(k_ref, t), 0.0)
            kv = lax.dot_general(
                key.T.astype(BF16), tile_of(v_ref, t).astype(BF16),
                (((1,), (0,)), ((), ())), preferred_element_type=F32,
            )
            kv = jnp.where(same, kv, 0.0)
            small = kv[:HEAD_DIM]
            for j in range(1, LANES // HEAD_DIM):
                small = small + kv[j * HEAD_DIM : (j + 1) * HEAD_DIM]
            state[t, :HEAD_DIM] = small
            state[t, HEAD_DIM:] = jnp.broadcast_to(jnp.sum(key, axis=0, keepdims=True), (ST - HEAD_DIM, LANES))
        for t in range(heads_tiles, state.shape[0]):
            state[t] = jnp.zeros((ST, LANES), F32)

    per = state.shape[0] // n_sp

    def share(dev):
        return pl.ds(dev * per, per)

    def scatter(off):
        peer = lax.rem(s + off, n_sp)
        return remote(state.at[share(peer)], rs_buf.at[off - 1], rs_ss.at[off - 1], rs_rs.at[off - 1], space=peer)

    def gather(off):
        peer = lax.rem(s + off, n_sp)
        return remote(prefix, full.at[off - 1], ag_ss.at[off - 1], ag_rs.at[off - 1], space=peer)


    def chain():
        return remote(prefix, pre_in, ch_ss, ch_rs, tm=next_id)

    def hop():
        total = state[share(s)]
        for off in range(1, n_sp):
            total = total + rs_buf[off - 1]

        @when(has_prev)
        def _():
            chain().wait_recv()
            prefix[...] = total + pre_in[...]

        @when(jnp.logical_not(has_prev))
        def _():
            prefix[...] = total

        when(has_next)(lambda: chain().start())
        for off in range(1, n_sp):
            gather(off).start()

    col = lax.broadcasted_iota(jnp.int32, (cols, LANES), 0)

    def conv(chunk):
        def tile(t, _):
            at = pl.ds(pl.multiple_of((spans[chunk][0] + t) * LANES, LANES), LANES)
            for vg in range(2):
                taps = []
                for a in range(3):
                    for b in range(3):
                        w = jnp.broadcast_to(sw_ref[a, b, vg : vg + 1, at], (cols, LANES))
                        if b == 0:
                            w = jnp.where(col == 0, 0.0, w)
                        if b == 2:
                            w = jnp.where(col == cols - 1, 0.0, w)
                        taps.append(w[None])
                above = hrecv[0, vg, :, at].astype(F32).reshape(frames, 1, cols, LANES)
                below = hrecv[1, vg, :, at].astype(F32).reshape(frames, 1, cols, LANES)
                for f in range(frames):
                    body = x_ref[vg, f, :, at].astype(F32).reshape(rows, cols, LANES)
                    ext = jnp.concatenate([above[f], body, below[f]], axis=0)
                    moved = [pltpu.roll(ext, 1, 1), ext, pltpu.roll(ext, cols - 1, 1)]
                    total = None
                    for a in range(3):
                        for b in range(3):
                            term = moved[b][a : a + rows] * taps[3 * a + b]
                            total = term if total is None else total + term
                    spat[vg, f, :, at] = total.reshape(rows * cols, LANES).astype(BF16)
            return 0

        lax.fori_loop(0, spans[chunk][1], tile, 0)

    def gate(chunk, before, now, into):
        def tile(t, _):
            at = pl.ds(pl.multiple_of((spans[chunk][0] + t) * LANES, LANES), LANES)
            mixed = []
            for vg in range(2):
                w = [tw_ref[j, vg : vg + 1, at] for j in range(3)]
                line = [now[vg, f, :, at].astype(F32) for f in range(frames)]
                if before is not None:
                    line = [before[vg, f, :, at].astype(F32) for f in (frames - 2, frames - 1)] + line
                    mixed.append([line[f] * w[0] + line[f + 1] * w[1] + line[f + 2] * w[2] for f in range(frames)])
                else:
                    got = []
                    for f in range(frames):
                        m = line[f] * w[2]
                        if f >= 1:
                            m = line[f - 1] * w[1] + m
                        if f >= 2:
                            m = line[f - 2] * w[0] + m
                        got.append(m)
                    mixed.append(got)
            for f in range(frames):
                v, g = mixed[0][f], mixed[1][f]
                into[f, :, at] = (v * (g / (1.0 + jnp.exp(-g)))).astype(BF16)
            return 0

        lax.fori_loop(0, spans[chunk][1], tile, 0)

    def ahead(chunk):
        part = (slice(None), slice(None), slice(None), lanes(chunk))
        return remote(spat.at[part], recv.at[part], m_ss.at[chunk], m_rs.at[chunk], tm=next_id)

    def back(chunk):
        part = (slice(None), slice(None), slice(None), lanes(chunk))
        return remote(spat.at[part], recv.at[part], m_ss.at[chunk], m_rs.at[chunk], tm=prev_id)

    def give(chunk):
        part = (slice(None), slice(None), lanes(chunk))
        return remote(outs.at[part], out_ref.at[part], o_ss.at[chunk], o_rs.at[chunk], tm=next_id)

    def finish_attention():
        for off in range(1, n_sp):
            gather(off).wait_recv()
        for t in range(heads_tiles):
            owner, local = t // per, t % per
            tile = prefix[local]
            for off in range(1, n_sp):
                tile = jnp.where(lax.rem(s + n_sp - off, n_sp) == owner, full[off - 1, local], tile)
            big = jnp.concatenate([tile[:HEAD_DIM]] * (LANES // HEAD_DIM), axis=0)
            keys = jnp.broadcast_to(tile[HEAD_DIM : HEAD_DIM + 1], (LANES, LANES)).T
            both = jnp.concatenate([jnp.where(same, big, 0.0), jnp.where(same, keys, 0.0)], axis=1)
            high = both.astype(BF16)
            low = (both - high.astype(F32)).astype(BF16)
            query = jnp.maximum(tile_of(q_ref, t), 0.0).astype(BF16)
            got = jnp.dot(query, high, preferred_element_type=F32) + jnp.dot(query, low, preferred_element_type=F32)
            value = (got[:, :LANES] / (got[:, LANES:] + 1.0)).astype(BF16)
            lo, hi = t * LANES, min(channels, (t + 1) * LANES)
            att_ref[:, lo:hi] = value[:, : hi - lo]

    sent_back = 0
    for place, chunk in enumerate(order):
        for side, cond in ((0, has_up), (1, has_down)):
            when(cond)(lambda chunk=chunk, side=side: halo_in(chunk, side).wait_recv())
        conv(chunk)
        if chunk in a_list[:2]:
            when(has_next)(lambda chunk=chunk: ahead(chunk).start())
        elif chunk in b_list and sent_back < AHEAD:
            when(has_prev)(lambda chunk=chunk: back(chunk).start())
            sent_back += 1
        if place == min(LATE, len(order) - 1):
            local_state()
            for off in range(1, n_sp):
                scatter(off).start()
        if place == min(LATE + 1, len(order) - 1):
            for off in range(1, n_sp):
                scatter(off).wait_recv()
            when(c == 0)(hop)

    @when(jnp.logical_not(has_prev))
    def _():
        for chunk in a_list:
            gate(chunk, None, spat, out_ref)

    for chunk in a_list[len(b_list) + 1 :]:
        when(has_next)(lambda chunk=chunk: ahead(chunk).start())
    finish = max(1, len(b_list) - 3)
    for i, chunk in enumerate(b_list):
        @when(jnp.logical_not(has_prev))
        def _():
            gate(chunk, None, spat, out_ref)

        @when(has_next)
        def _():
            back(chunk).wait_recv()
            gate(chunk, spat, recv, outs)
            give(chunk).start()

        @when(has_prev)
        def _():
            back(chunk).wait_send()
            if i + AHEAD < len(b_list):
                back(b_list[i + AHEAD]).start()

        if 2 <= i + 1 < len(a_list):
            when(has_next)(lambda i=i: ahead(a_list[i + 1]).start())
        if i == finish:
            when(jnp.logical_and(has_prev, c >= i))(hop)
            finish_attention()
        elif 1 <= i < finish:
            when(c == i)(hop)
        if 2 <= i < len(b_list) - 1 and i - 2 < len(a_list):
            @when(has_prev)
            def _():
                ahead(a_list[i - 2]).wait_recv()
                gate(a_list[i - 2], recv, spat, out_ref)

    done = max(0, min(len(a_list), len(b_list) - 3))

    @when(has_prev)
    def _():
        for chunk in a_list[done:]:
            ahead(chunk).wait_recv()
            gate(chunk, recv, spat, out_ref)
        for chunk in b_list:
            give(chunk).wait_recv()

    @when(has_next)
    def _():
        for chunk in a_list:
            ahead(chunk).wait_send()
        for chunk in b_list:
            give(chunk).wait_send()
        chain().wait_send()

    for off in range(1, n_sp):
        scatter(off).wait_send()
        gather(off).wait_send()
    for chunk in order:
        for way, cond in ((0, has_up), (1, has_down)):
            when(cond)(lambda chunk=chunk, way=way: halo(chunk, way).wait_send())


def cut(total, most):
    count = -(-total // most)
    return [total // count + (1 if i < total % count else 0) for i in range(count)]


def plan_of(n_tm, n_sp, tiles):
    forward = max(1, round(tiles * A_SHARE))
    a_sizes = [1] + cut(forward - 1, CHUNK) if forward > 1 else [forward]
    rest = tiles - forward
    b_sizes = [1, 2] + cut(rest - 6, B_CHUNK) + [2, 1] if rest >= 8 else [1] * rest
    spans, at = [], 0
    for size in a_sizes + b_sizes:
        spans.append((at, size))
        at += size
    a_list = list(range(len(a_sizes)))
    b_list = list(range(len(a_sizes), len(spans)))
    order = []
    for i in range(max(len(a_list), len(b_list))):
        order += b_list[i : i + 1] + a_list[i : i + 1]
    return n_tm, n_sp, order, a_list, b_list, spans


def on_device(query_proj, key_proj, value_proj, expanded, spatial_weight, temporal_weight):
    n_tm, n_sp = lax.axis_size("tm"), lax.axis_size("space")
    frames, rows, cols, channels = query_proj.shape
    hidden = expanded.shape[-1]
    tiles = -(-hidden // LANES)
    padded = tiles * LANES
    extra = padded - hidden
    tokens = frames * rows * cols
    x = jnp.pad(expanded.transpose(3, 0, 1, 2, 4), ((0, 0),) * 4 + ((0, extra),))
    x = x.reshape(2, frames, rows * cols, padded)
    sw = jnp.pad(spatial_weight, ((0, 0),) * 3 + ((0, extra),))
    tw = jnp.pad(temporal_weight, ((0, 0),) * 2 + ((0, extra),))
    per = -(-(-(-channels // LANES)) // n_sp)
    plan = plan_of(n_tm, n_sp, tiles)
    chunks = len(plan[-1])
    dma = pltpu.SemaphoreType.DMA
    vmem = pl.BlockSpec(memory_space=pltpu.VMEM)
    att, out = pl.pallas_call(
        functools.partial(kernel, plan),
        out_shape=(
            jax.ShapeDtypeStruct((tokens, channels), BF16),
            jax.ShapeDtypeStruct((frames, rows * cols, padded), BF16),
        ),
        in_specs=[vmem] * 6,
        out_specs=(vmem, vmem),
        scratch_shapes=[
            pltpu.VMEM((2, frames, rows * cols, padded), BF16),
            pltpu.VMEM((2, frames, rows * cols, padded), BF16),
            pltpu.VMEM((frames, rows * cols, padded), BF16),
            pltpu.VMEM((2, 2, frames * cols, padded), BF16),
            pltpu.VMEM((2, 2, frames * cols, padded), BF16),
            pltpu.VMEM((per * n_sp, ST, LANES), F32),
            pltpu.VMEM((n_sp - 1, per, ST, LANES), F32),
            pltpu.VMEM((per, ST, LANES), F32),
            pltpu.VMEM((per, ST, LANES), F32),
            pltpu.VMEM((n_sp - 1, per, ST, LANES), F32),
            dma((2, chunks)), dma((2, chunks)),
            dma((chunks,)), dma((chunks,)),
            dma((chunks,)), dma((chunks,)),
            dma((n_sp - 1,)), dma((n_sp - 1,)),
            dma((n_sp - 1,)), dma((n_sp - 1,)),
            dma, dma,
        ],
        compiler_params=pltpu.CompilerParams(
            collective_id=0, has_side_effects=True, vmem_limit_bytes=40 * 1024 * 1024
        ),
    )(
        query_proj.reshape(tokens, channels),
        key_proj.reshape(tokens, channels),
        value_proj.reshape(tokens, channels),
        x, sw, tw,
    )
    attended = att.reshape(frames, rows, cols, channels)
    gated = out.reshape(frames, rows, cols, padded)[..., :hidden]
    return attended, gated


def solution(mesh):
    token = P(("groups", "tm"), "space", None, "mp")
    return jax.shard_map(
        on_device,
        mesh=mesh,
        in_specs=(
            token, token, token,
            P(("groups", "tm"), "space", None, None, "mp"),
            P(None, None, None, "mp"),
            P(None, None, "mp"),
        ),
        out_specs=(token, token),
        check_vma=False,
    )
```
